32 devices in a mesh: cuts: 4 (over y, core), bita: 4 (over z), bitb: 2 (over x).
Axes of the slice: x: 2, y: 2, z: 4, core: 2. Of those that a mesh axis runs over, the one named last changes fastest.
Arguments:
- slice_tensors: bfloat16 [4, 2, 4, 2, 512, 256], P('cuts', None, 'bita', 'bitb'), may hold values from -4 to 4
- slice_gates: bfloat16 [4, 2, 2, 256, 256], P('cuts'), may hold values from -0.25 to 0.25
- last_gate: bfloat16 [2, 256, 256], replicated, may hold values from -0.25 to 0.25
- mix_first: float32 [2, 4, 4], replicated, may hold values from -2 to 2
- mix_second: float32 [2, 2, 2], replicated, may hold values from -3 to 3
- mix_joint: float32 [2, 8, 8], replicated, may hold values from -1.5 to 1.5
Outputs:
- amplitudes: float32 [2, 4, 2, 8, 64, 256], P(None, 'bita', 'bitb', None, 'cuts')
The draws below stay inside these ranges and needn't reach their ends.
All inputs are finite; a program needn't handle non-finite values.
Results may differ from the reference program's by a relative error of at most 0.013.
Values may be sent and summed in bfloat16 or wider, within the bound.
A program may use at most 64 MiB of HBM per device.

```python
import jax
import jax.numpy as jnp
from jax import lax

K = 256
ROWS = 512
SLICES = 4
GROUP = 8
N_BITA = 4
N_BITB = 2


def steps_of(key, extent, cuts, least, high):
    level = 1.0
    for dim, blocks in cuts:
        steps = jax.random.uniform(jax.random.fold_in(jax.random.fold_in(key, 6), dim), (blocks,), jnp.float32, least / len(cuts), high / len(cuts))
        level = level * jnp.repeat(jnp.exp(steps), extent[dim] // blocks).reshape((-1,) + (1,) * (len(extent) - 1 - dim))
    return level


def normal_values(rng, dims, scale, most, split=(), held_as=jnp.bfloat16):
    drawn = jax.random.normal(rng, dims, jnp.float32) * scale
    if len(split) > 0:
        drawn = steps_of(rng, dims, split, -0.22, 0.18) * drawn
    return jnp.clip(drawn, min=-most, max=most).astype(held_as)


def setup_inputs(seed: int = 0) -> dict:
    splits = jax.random.split(jax.random.key(seed), 7)
    return {
        "slice_tensors": normal_values(splits[0], (SLICES, 2, N_BITA, N_BITB, ROWS, K), 0.25, 4.0, ((0, 4), (2, 4), (3, 2))),
        "slice_gates": normal_values(splits[1], (SLICES, 2, 2, K, K), (2 * K) ** -0.5, 0.25, ((0, 4),)),
        "last_gate": normal_values(splits[2], (2, K, K), (2 * K) ** -0.5, 0.25),
        "mix_first": normal_values(splits[3], (2, N_BITA, N_BITA), (2 * N_BITA) ** -0.5, 2.0, (), jnp.float32),
        "mix_second": normal_values(splits[4], (2, N_BITB, N_BITB), (2 * N_BITB) ** -0.5, 3.0, (), jnp.float32),
        "mix_joint": normal_values(splits[5], (2, GROUP, GROUP), (2 * GROUP) ** -0.5, 1.5, (), jnp.float32),
    }


def mix_group(values, matrix):
    return jnp.einsum("...csm,cd->...dsm", values, matrix, precision=lax.Precision.HIGHEST)


def contract(tensor, gate_pair, mixing):
    products = jnp.einsum("z...k,wkm->zw...m", tensor.astype(jnp.float32), gate_pair.astype(jnp.float32), precision=lax.Precision.HIGHEST)
    real_part = products[0, 0] - products[1, 1]
    imag_part = products[0, 1] + products[1, 0]
    out_real = mix_group(real_part, mixing[0]) - mix_group(imag_part, mixing[1])
    out_imag = mix_group(real_part, mixing[1]) + mix_group(imag_part, mixing[0])
    return jnp.stack([out_real, out_imag])


def reference(slice_tensors, slice_gates, last_gate, mix_first, mix_second, mix_joint):
    joint = N_BITA * N_BITB

    def one_slice(tensor, own_gates):
        swapped = tensor.reshape(2, N_BITA, N_BITB, N_BITA, ROWS // N_BITA, K).transpose(0, 3, 2, 1, 4, 5)
        first = contract(swapped, own_gates[0], mix_first).astype(jnp.bfloat16)
        swapped = first.reshape(2, N_BITA, N_BITB, N_BITB, ROWS // N_BITB, K).transpose(0, 1, 3, 2, 4, 5)
        second = contract(swapped, own_gates[1], mix_second).astype(jnp.bfloat16)
        swapped = second.reshape(2, joint, joint, ROWS // joint, K).transpose(0, 2, 1, 3, 4)
        return contract(swapped, last_gate, mix_joint)

    def add_slice(carry, pieces):
        return carry + one_slice(pieces[0], pieces[1]), None

    start = jnp.zeros((2, joint, joint, ROWS // joint, K), jnp.float32)
    amplitudes, unused = lax.scan(add_slice, start, (slice_tensors, slice_gates))
    return amplitudes.reshape(2, N_BITA, N_BITB, joint, ROWS // joint, K)
```

```python
import functools

import jax
import jax.numpy as jnp
from jax import lax
from jax.experimental import pallas as pl
from jax.experimental.pallas import tpu as pltpu
from jax.sharding import PartitionSpec as P

MESH = pl.DeviceIdType.MESH
BF16 = jnp.bfloat16
F32 = jnp.float32


def mix_group(values, matrix):
    return jnp.einsum("...csm,cd->...dsm", values, matrix, precision=lax.Precision.HIGHEST)


def contract(tensor, gate_pair, mixing):
    products = jnp.einsum(
        "z...k,wkm->zw...m", tensor, gate_pair, preferred_element_type=jnp.float32
    )
    real_part = products[0, 0] - products[1, 1]
    imag_part = products[0, 1] + products[1, 0]
    out_real = mix_group(real_part, mixing[0]) - mix_group(imag_part, mixing[1])
    out_imag = mix_group(real_part, mixing[1]) + mix_group(imag_part, mixing[0])
    return jnp.stack([out_real, out_imag])


def by_collectives(slice_tensors, slice_gates, last_gate, mix_first, mix_second, mix_joint):
    row_count = slice_tensors.shape[4]
    width_k = slice_tensors.shape[5]
    bita_size = lax.axis_size("bita")
    bitb_size = lax.axis_size("bitb")
    joint_size = bita_size * bitb_size
    own_gates = slice_gates[0]
    tensor = slice_tensors.reshape(2, bita_size, row_count // bita_size, width_k)
    tensor = lax.all_to_all(tensor, "bita", split_axis=1, concat_axis=1, tiled=True)
    tensor = contract(tensor, own_gates[0], mix_first).astype(jnp.bfloat16)
    tensor = tensor.reshape(2, bitb_size, row_count // bitb_size, width_k)
    tensor = lax.all_to_all(tensor, "bitb", split_axis=1, concat_axis=1, tiled=True)
    tensor = contract(tensor, own_gates[1], mix_second).astype(jnp.bfloat16)
    tensor = lax.all_to_all(
        tensor.reshape(2, joint_size, row_count // joint_size, width_k),
        ("bita", "bitb"),
        split_axis=1,
        concat_axis=1,
        tiled=True,
    )
    result = contract(tensor, last_gate, mix_joint)
    amplitudes = lax.psum_scatter(result, "cuts", scatter_dimension=2, tiled=True)
    return amplitudes.reshape(2, 1, 1, joint_size, amplitudes.shape[2], width_k)


def dot(a, b):
    return jnp.dot(a, b, preferred_element_type=F32)


def wide(real, imag):
    return (
        jnp.concatenate([real, imag], axis=1),
        jnp.concatenate([-imag, real], axis=1),
    )


def kernel(
    x_ref, gates_ref, last_ref, m1_ref, m2_ref, mj_ref, out_ref,
    send_a, recv_a, send_b, recv_b, send_c, recv_c, send_d, recv_d,
    a_send_sem, a_recv_sem, b_send_sem, b_recv_sem,
    c_send_sem, c_recv_sem, d_send_sem, d_recv_sem,
):
    cut = lax.axis_index("cuts")
    bita = lax.axis_index("bita")
    bitb = lax.axis_index("bitb")
    na, nb = 4, 2
    width = x_ref.shape[5]
    rows = x_ref.shape[4]
    fine = out_ref.shape[4]
    y, core = cut // 2, lax.rem(cut, 2)
    at_core = y * 2 + (1 - core)
    at_y = (1 - y) * 2 + core
    to_core = (at_core, bita, bitb)
    to_y = (at_y, bita, bitb)
    to_x = (cut, bita, 1 - bitb)
    to_z = [(cut, lax.rem(bita + d, na), bitb) for d in range(1, na)]

    barrier = pltpu.get_barrier_semaphore()
    for device in [to_core, to_y, to_x] + to_z:
        pl.semaphore_signal(barrier, inc=1, device_id=device, device_id_type=MESH)

    g1 = wide(gates_ref[0, 1, 0], gates_ref[0, 1, 1])
    both = dot(gates_ref[0, 0, 0], g1[0]) + dot(gates_ref[0, 0, 1], g1[1])
    both = both.astype(BF16)
    gate = wide(both[:, :width], both[:, width:])

    def product(target, halves):
        parts = []
        for z in range(2):
            pieces = []
            for half in halves:
                for u in range(na):
                    start = u * (rows // na) + half * (rows // na // nb) + target * fine
                    pieces.append(x_ref[0, z, 0, 0, pl.ds(pl.multiple_of(start, 16), fine), :])
            parts.append(jnp.concatenate(pieces, axis=0))
        return dot(parts[0], gate[0]) + dot(parts[1], gate[1])

    halves = (1 - bitb, bitb)
    part = na * fine

    def remote(src, dst, send_sem, recv_sem, device):
        return pltpu.make_async_remote_copy(
            src_ref=src, dst_ref=dst, send_sem=send_sem, recv_sem=recv_sem,
            device_id=device, device_id_type=MESH,
        )

    a_copies, b_copies, d_copies = [], [], []
    for i, target in enumerate(((1 - y) * 2 + (1 - core), y * 2 + (1 - core))):
        send_a[i] = product(target, halves).astype(BF16)
        if i == 0:
            pl.semaphore_wait(barrier, 6)
        copy = remote(send_a.at[i], recv_a.at[i], a_send_sem.at[i], a_recv_sem.at[i], to_core)
        copy.start()
        a_copies.append(copy)

    total = product(at_y, halves)
    a_copies[0].wait_recv()
    for q in range(nb):
        rows_q = slice(q * part, (q + 1) * part)
        send_b[q] = (total[rows_q] + recv_a[0, rows_q].astype(F32)).astype(BF16)
        copy = remote(send_b.at[q], recv_b.at[q], b_send_sem.at[q], b_recv_sem.at[q], to_y)
        copy.start()
        b_copies.append(copy)
    total = product(cut, halves)
    a_copies[1].wait_recv()
    total = total + recv_a[1].astype(F32)

    b_copies[0].wait_recv()
    send_c[...] = (total[:part] + recv_b[0].astype(F32)).astype(BF16)
    c_copy = remote(send_c, recv_c, c_send_sem.at[0], c_recv_sem.at[0], to_x)
    c_copy.start()

    low = lax.rem(bita, 2)
    lanes = na * na * fine
    w_id = lax.broadcasted_iota(jnp.int32, (na * nb, lanes), 0)
    lane = lax.broadcasted_iota(jnp.int32, (na * nb, lanes), 1)
    u_id = lax.rem(lane // fine, na)
    d_id = lane // (fine * na)
    mixed = [jnp.zeros((na * nb, lanes), F32), jnp.zeros((na * nb, lanes), F32)]
    for b in range(nb):
        first, joint = [], []
        for z in range(2):
            a_part = jnp.zeros((na * nb, lanes), F32)
            for d in range(na):
                a_part = jnp.where(d_id == d, m1_ref[z, lax.rem(bita + d, na), b * 2 + low], a_part)
            j_part = jnp.zeros((na * nb, lanes), F32)
            for u in range(na):
                for w in range(na * nb):
                    j_part = jnp.where((u_id == u) & (w_id == w), mj_ref[z, u * nb + b, w], j_part)
            first.append(a_part)
            joint.append(j_part)
        mixed[0] += first[0] * joint[0] - first[1] * joint[1]
        mixed[1] += first[0] * joint[1] + first[1] * joint[0]
    same = lax.rem(
        lax.broadcasted_iota(jnp.int32, (fine, lanes), 1), fine
    ) == lax.broadcasted_iota(jnp.int32, (fine, lanes), 0)
    spread = []
    for z in range(2):
        spread.append(jnp.concatenate(
            [jnp.where(same, mixed[z][w:w + 1], 0.0) for w in range(na * nb)], axis=0
        ).astype(BF16))
    last = wide(last_ref[0], last_ref[1])

    b_copies[1].wait_recv()
    own = total[part:] + recv_b[1].astype(F32)
    own_r, own_i = own[:, :width], own[:, width:]
    c_copy.wait_recv()
    other = recv_c[...].astype(F32)
    other_r, other_i = other[:, :width], other[:, width:]
    for v in range(nb):
        kr, ki = m2_ref[0, bitb, v], m2_ref[1, bitb, v]
        pr, pi = m2_ref[0, 1 - bitb, v], m2_ref[1, 1 - bitb, v]
        send_d[v] = jnp.concatenate([
            own_r * kr - own_i * ki + other_r * pr - other_i * pi,
            own_r * ki + own_i * kr + other_r * pi + other_i * pr,
        ], axis=1).astype(BF16)
    for d in range(1, na):
        to = lax.rem(bita + d, na)
        copy = remote(
            send_d.at[to // 2], recv_d.at[na - 1 - d], d_send_sem.at[d - 1],
            d_recv_sem.at[na - 1 - d], (cut, to, bitb),
        )
        copy.start()
        d_copies.append(copy)

    def piece(s, value):
        columns = slice(s * part, (s + 1) * part)
        return dot(spread[0][:, columns], value), dot(spread[1][:, columns], value)

    sum_r, sum_i = piece(0, send_d[bita // 2])
    for s in range(1, na):
        d_copies[na - 1 - s].wait_recv()
        more = piece(s, recv_d[s - 1])
        sum_r += more[0]
        sum_i += more[1]
    real = (sum_r[:, :width] - sum_i[:, width:]).astype(BF16)
    imag = (sum_r[:, width:] + sum_i[:, :width]).astype(BF16)
    result = dot(real, last[0]) + dot(imag, last[1])
    for z in range(2):
        out_ref[z, 0, 0] = result[:, z * width:(z + 1) * width].reshape(na * nb, fine, width)
    for copy in a_copies + b_copies + [c_copy] + d_copies:
        copy.wait_send()


def by_kernel(slice_tensors, slice_gates, last_gate, mix_first, mix_second, mix_joint):
    rows, width = slice_tensors.shape[4:]
    na, nb, cuts = lax.axis_size("bita"), lax.axis_size("bitb"), lax.axis_size("cuts")
    fine = rows // (na * nb * cuts)
    part = na * fine
    vmem = pl.BlockSpec(memory_space=pltpu.VMEM)
    smem = pl.BlockSpec(memory_space=pltpu.SMEM)
    dma = pltpu.SemaphoreType.DMA
    return pl.pallas_call(
        kernel,
        out_shape=jax.ShapeDtypeStruct((2, 1, 1, na * nb, fine, width), F32),
        in_specs=[vmem] * 3 + [smem] * 3,
        out_specs=vmem,
        scratch_shapes=[
            pltpu.VMEM((2, nb * part, 2 * width), BF16),
            pltpu.VMEM((2, nb * part, 2 * width), BF16),
            pltpu.VMEM((nb, part, 2 * width), BF16),
            pltpu.VMEM((nb, part, 2 * width), BF16),
            pltpu.VMEM((part, 2 * width), BF16),
            pltpu.VMEM((part, 2 * width), BF16),
            pltpu.VMEM((nb, part, 2 * width), BF16),
            pltpu.VMEM((na - 1, part, 2 * width), BF16),
            dma((2,)), dma((2,)), dma((2,)), dma((2,)),
            dma((1,)), dma((1,)), dma((na - 1,)), dma((na - 1,)),
        ],
        compiler_params=pltpu.CompilerParams(
            collective_id=0, has_side_effects=True, vmem_limit_bytes=32 * 2**20
        ),
    )(slice_tensors, slice_gates, last_gate, mix_first, mix_second, mix_joint)


def solution(mesh):
    placed = (
        P("cuts", None, "bita", "bitb", None, None),
        P("cuts", None, None, None, None),
        P(),
        P(),
        P(),
        P(),
    )
    pairs = (mesh.shape["cuts"], mesh.shape["bita"], mesh.shape["bitb"]) == (4, 4, 2)
    return jax.shard_map(
        by_kernel if pairs else by_collectives,
        mesh=mesh,
        in_specs=placed,
        out_specs=P(None, "bita", "bitb", None, "cuts", None),
        check_vma=False,
    )
```

```python
import functools

import jax
import jax.numpy as jnp
from jax import lax
from jax.experimental import pallas as pl
from jax.experimental.pallas import tpu as pltpu
from jax.sharding import PartitionSpec as P

MESH = pl.DeviceIdType.MESH
BF16 = jnp.bfloat16
F32 = jnp.float32


def mix_group(values, matrix):
    return jnp.einsum("...csm,cd->...dsm", values, matrix, precision=lax.Precision.HIGHEST)


def contract(tensor, gate_pair, mixing):
    products = jnp.einsum(
        "z...k,wkm->zw...m", tensor, gate_pair, preferred_element_type=jnp.float32
    )
    real_part = products[0, 0] - products[1, 1]
    imag_part = products[0, 1] + products[1, 0]
    out_real = mix_group(real_part, mixing[0]) - mix_group(imag_part, mixing[1])
    out_imag = mix_group(real_part, mixing[1]) + mix_group(imag_part, mixing[0])
    return jnp.stack([out_real, out_imag])


def by_collectives(slice_tensors, slice_gates, last_gate, mix_first, mix_second, mix_joint):
    row_count = slice_tensors.shape[4]
    width_k = slice_tensors.shape[5]
    bita_size = lax.axis_size("bita")
    bitb_size = lax.axis_size("bitb")
    joint_size = bita_size * bitb_size
    own_gates = slice_gates[0]
    tensor = slice_tensors.reshape(2, bita_size, row_count // bita_size, width_k)
    tensor = lax.all_to_all(tensor, "bita", split_axis=1, concat_axis=1, tiled=True)
    tensor = contract(tensor, own_gates[0], mix_first).astype(jnp.bfloat16)
    tensor = tensor.reshape(2, bitb_size, row_count // bitb_size, width_k)
    tensor = lax.all_to_all(tensor, "bitb", split_axis=1, concat_axis=1, tiled=True)
    tensor = contract(tensor, own_gates[1], mix_second).astype(jnp.bfloat16)
    tensor = lax.all_to_all(
        tensor.reshape(2, joint_size, row_count // joint_size, width_k),
        ("bita", "bitb"),
        split_axis=1,
        concat_axis=1,
        tiled=True,
    )
    result = contract(tensor, last_gate, mix_joint)
    amplitudes = lax.psum_scatter(result, "cuts", scatter_dimension=2, tiled=True)
    return amplitudes.reshape(2, 1, 1, joint_size, amplitudes.shape[2], width_k)


def dot(a, b):
    return jnp.dot(a, b, preferred_element_type=F32)


def wide(real, imag):
    return (
        jnp.concatenate([real, imag], axis=1),
        jnp.concatenate([-imag, real], axis=1),
    )


def kernel(
    x_hbm, gates_hbm, last_hbm, m1_hbm, m2_hbm, mj_hbm, out_ref,
    x_ref, gates_ref, last_ref, m1_ref, m2_ref, mj_ref,
    send_a, recv_a, send_b, recv_b, send_c, recv_c, send_d, recv_d,
    load_sem, a_send_sem, a_recv_sem, b_send_sem, b_recv_sem,
    c_send_sem, c_recv_sem, d_send_sem, d_recv_sem,
):
    cut = lax.axis_index("cuts")
    bita = lax.axis_index("bita")
    bitb = lax.axis_index("bitb")
    na, nb = 4, 2
    _, rows, width = x_ref.shape
    fine = out_ref.shape[4]
    y, core = cut // 2, lax.rem(cut, 2)
    at_core = y * 2 + (1 - core)
    at_y = (1 - y) * 2 + core
    to_core = (at_core, bita, bitb)
    to_y = (at_y, bita, bitb)
    to_x = (cut, bita, 1 - bitb)
    to_z = [(cut, lax.rem(bita + d, na), bitb) for d in range(1, na)]

    def load(src, dst, i):
        copy = pltpu.make_async_copy(src, dst, load_sem.at[i])
        copy.start()
        return copy

    load_gates = [load(gates_hbm.at[0, i], gates_ref.at[i], i) for i in (1, 0)]
    load_x = [load(x_hbm.at[0, z, 0, 0], x_ref.at[z], 2 + z) for z in range(2)]
    load_rest = [
        load(src, dst, 4 + i)
        for i, (src, dst) in enumerate((
            (m1_hbm, m1_ref), (m2_hbm, m2_ref), (mj_hbm, mj_ref), (last_hbm, last_ref)
        ))
    ]

    barrier = pltpu.get_barrier_semaphore()
    for device in [to_core, to_y, to_x] + to_z:
        pl.semaphore_signal(barrier, inc=1, device_id=device, device_id_type=MESH)

    for copy in load_gates:
        copy.wait()
    g1 = wide(gates_ref[1, 0], gates_ref[1, 1])
    both = dot(gates_ref[0, 0], g1[0]) + dot(gates_ref[0, 1], g1[1])
    both = both.astype(BF16)
    gate = wide(both[:, :width], both[:, width:])
    for copy in load_x:
        copy.wait()

    chunks = ((0, 2), (1, 3))
    halves = (1 - bitb, bitb)
    part = 2 * fine

    def product(target):
        parts = []
        for z in range(2):
            pieces = []
            for half in halves:
                for chunk in chunks:
                    for u in chunk:
                        start = u * (rows // na) + half * (rows // na // nb) + target * fine
                        pieces.append(x_ref[z, pl.ds(pl.multiple_of(start, 16), fine), :])
            parts.append(jnp.concatenate(pieces, axis=0))
        return dot(parts[0], gate[0]) + dot(parts[1], gate[1])

    def remote(src, dst, send_sem, recv_sem, device):
        return pltpu.make_async_remote_copy(
            src_ref=src, dst_ref=dst, send_sem=send_sem, recv_sem=recv_sem,
            device_id=device, device_id_type=MESH,
        )

    a_copies, b_copies, c_copies, d_copies = [], [], [], []
    for i, target in enumerate(((1 - y) * 2 + (1 - core), y * 2 + (1 - core))):
        send_a[i] = product(target).astype(BF16)
        if i == 0:
            pl.semaphore_wait(barrier, 6)
        copy = remote(send_a.at[i], recv_a.at[i], a_send_sem.at[i], a_recv_sem.at[i], to_core)
        copy.start()
        a_copies.append(copy)

    total = product(at_y)
    a_copies[0].wait_recv()
    for q in range(4):
        rows_q = slice(q * part, (q + 1) * part)
        send_b[q] = (total[rows_q] + recv_a[0, rows_q].astype(F32)).astype(BF16)
        copy = remote(send_b.at[q], recv_b.at[q], b_send_sem.at[q], b_recv_sem.at[q], to_y)
        copy.start()
        b_copies.append(copy)
    total = product(cut)
    a_copies[1].wait_recv()
    total = total + recv_a[1].astype(F32)

    def summed(q):
        b_copies[q].wait_recv()
        return total[q * part:(q + 1) * part] + recv_b[q].astype(F32)

    for copy in load_rest:
        copy.wait()
    low = lax.rem(bita, 2)
    lanes = na * na * fine
    by_fine = fine.bit_length() - 1
    w_id = lax.broadcasted_iota(jnp.int32, (na * nb, lanes), 0)
    lane = lax.broadcasted_iota(jnp.int32, (na * nb, lanes), 1)
    u_id = (((lane >> by_fine) & 1) << 1) | (lane >> (by_fine + 3))
    d_id = (lane >> (by_fine + 1)) & 3
    mixed = [jnp.zeros((na * nb, lanes), F32), jnp.zeros((na * nb, lanes), F32)]
    for b in range(nb):
        first, joint = [], []
        for z in range(2):
            a_part = jnp.zeros((na * nb, lanes), F32)
            for d in range(na):
                a_part = jnp.where(d_id == d, m1_ref[z, lax.rem(bita + d, na), b * 2 + low], a_part)
            j_part = jnp.zeros((na * nb, lanes), F32)
            for u in range(na):
                for w in range(na * nb):
                    j_part = jnp.where((u_id == u) & (w_id == w), mj_ref[z, u * nb + b, w], j_part)
            first.append(a_part)
            joint.append(j_part)
        mixed[0] += first[0] * joint[0] - first[1] * joint[1]
        mixed[1] += first[0] * joint[1] + first[1] * joint[0]

    for h in range(2):
        send_c[h] = summed(h).astype(BF16)
        copy = remote(send_c.at[h], recv_c.at[h], c_send_sem.at[h], c_recv_sem.at[h], to_x)
        copy.start()
        c_copies.append(copy)

    same = (
        lax.broadcasted_iota(jnp.int32, (fine, lanes), 1) & (fine - 1)
    ) == lax.broadcasted_iota(jnp.int32, (fine, lanes), 0)
    spread = jnp.concatenate([
        jnp.where(same, mixed[z][w:w + 1], 0.0) for z in range(2) for w in range(na * nb)
    ], axis=0).astype(BF16)
    last = wide(last_ref[0], last_ref[1])

    for h in range(2):
        own = summed(2 + h)
        own_r, own_i = own[:, :width], own[:, width:]
        c_copies[h].wait_recv()
        other = recv_c[h].astype(F32)
        other_r, other_i = other[:, :width], other[:, width:]
        for v in range(nb):
            kr, ki = m2_ref[0, bitb, v], m2_ref[1, bitb, v]
            pr, pi = m2_ref[0, 1 - bitb, v], m2_ref[1, 1 - bitb, v]
            send_d[h, v] = jnp.concatenate([
                own_r * kr - own_i * ki + other_r * pr - other_i * pi,
                own_r * ki + own_i * kr + other_r * pi + other_i * pr,
            ], axis=1).astype(BF16)
        for d in (2, 1, 3):
            to = lax.rem(bita + d, na)
            copy = remote(
                send_d.at[h, to // 2], recv_d.at[h, na - 1 - d], d_send_sem.at[h, d - 1],
                d_recv_sem.at[h, na - 1 - d], (cut, to, bitb),
            )
            copy.start()
            d_copies.append(copy)

    columns = na * part
    sums = None
    for h in range(2):
        for copy in d_copies[h * (na - 1):(h + 1) * (na - 1)]:
            copy.wait_recv()
        value = jnp.concatenate(
            [send_d[h, bita // 2]] + [recv_d[h, s] for s in range(na - 1)], axis=0
        )
        more = dot(spread[:, h * columns:(h + 1) * columns], value)
        sums = more if sums is None else sums + more
    count = na * nb * fine
    real = (sums[:count, :width] - sums[count:, width:]).astype(BF16)
    imag = (sums[:count, width:] + sums[count:, :width]).astype(BF16)
    result = dot(real, last[0]) + dot(imag, last[1])
    for z in range(2):
        out_ref[z, 0, 0] = result[:, z * width:(z + 1) * width].reshape(na * nb, fine, width)
    for copy in a_copies + b_copies + c_copies + d_copies:
        copy.wait_send()


def by_kernel(slice_tensors, slice_gates, last_gate, mix_first, mix_second, mix_joint):
    rows, width = slice_tensors.shape[4:]
    na, nb, cuts = lax.axis_size("bita"), lax.axis_size("bitb"), lax.axis_size("cuts")
    fine = rows // (na * nb * cuts)
    part = 2 * fine
    hbm = pl.BlockSpec(memory_space=pltpu.MemorySpace.HBM)
    dma = pltpu.SemaphoreType.DMA
    return pl.pallas_call(
        kernel,
        out_shape=jax.ShapeDtypeStruct((2, 1, 1, na * nb, fine, width), F32),
        in_specs=[hbm] * 6,
        out_specs=pl.BlockSpec(memory_space=pltpu.VMEM),
        scratch_shapes=[
            pltpu.VMEM((2, rows, width), BF16),
            pltpu.VMEM(slice_gates.shape[1:], BF16),
            pltpu.VMEM(last_gate.shape, BF16),
            pltpu.SMEM(mix_first.shape, F32),
            pltpu.SMEM(mix_second.shape, F32),
            pltpu.SMEM(mix_joint.shape, F32),
            pltpu.VMEM((2, 4 * part, 2 * width), BF16),
            pltpu.VMEM((2, 4 * part, 2 * width), BF16),
            pltpu.VMEM((4, part, 2 * width), BF16),
            pltpu.VMEM((4, part, 2 * width), BF16),
            pltpu.VMEM((2, part, 2 * width), BF16),
            pltpu.VMEM((2, part, 2 * width), BF16),
            pltpu.VMEM((2, nb, part, 2 * width), BF16),
            pltpu.VMEM((2, na - 1, part, 2 * width), BF16),
            dma((8,)), dma((2,)), dma((2,)), dma((4,)), dma((4,)),
            dma((2,)), dma((2,)), dma((2, na - 1)), dma((2, na - 1)),
        ],
        compiler_params=pltpu.CompilerParams(
            collective_id=0, has_side_effects=True, vmem_limit_bytes=32 * 2**20
        ),
    )(slice_tensors, slice_gates, last_gate, mix_first, mix_second, mix_joint)


def solution(mesh):
    placed = (
        P("cuts", None, "bita", "bitb", None, None),
        P("cuts", None, None, None, None),
        P(),
        P(),
        P(),
        P(),
    )
    pairs = (mesh.shape["cuts"], mesh.shape["bita"], mesh.shape["bitb"]) == (4, 4, 2)
    return jax.shard_map(
        by_kernel if pairs else by_collectives,
        mesh=mesh,
        in_specs=placed,
        out_specs=P(None, "bita", "bitb", None, "cuts", None),
        check_vma=False,
    )
```

```python
import functools

import jax
import jax.numpy as jnp
from jax import lax
from jax.experimental import pallas as pl
from jax.experimental.pallas import tpu as pltpu
from jax.sharding import PartitionSpec as P

MESH = pl.DeviceIdType.MESH
BF16 = jnp.bfloat16
F32 = jnp.float32


def mix_group(values, matrix):
    return jnp.einsum("...csm,cd->...dsm", values, matrix, precision=lax.Precision.HIGHEST)


def contract(tensor, gate_pair, mixing):
    products = jnp.einsum(
        "z...k,wkm->zw...m", tensor, gate_pair, preferred_element_type=jnp.float32
    )
    real_part = products[0, 0] - products[1, 1]
    imag_part = products[0, 1] + products[1, 0]
    out_real = mix_group(real_part, mixing[0]) - mix_group(imag_part, mixing[1])
    out_imag = mix_group(real_part, mixing[1]) + mix_group(imag_part, mixing[0])
    return jnp.stack([out_real, out_imag])


def by_collectives(slice_tensors, slice_gates, last_gate, mix_first, mix_second, mix_joint):
    row_count = slice_tensors.shape[4]
    width_k = slice_tensors.shape[5]
    bita_size = lax.axis_size("bita")
    bitb_size = lax.axis_size("bitb")
    joint_size = bita_size * bitb_size
    own_gates = slice_gates[0]
    tensor = slice_tensors.reshape(2, bita_size, row_count // bita_size, width_k)
    tensor = lax.all_to_all(tensor, "bita", split_axis=1, concat_axis=1, tiled=True)
    tensor = contract(tensor, own_gates[0], mix_first).astype(jnp.bfloat16)
    tensor = tensor.reshape(2, bitb_size, row_count // bitb_size, width_k)
    tensor = lax.all_to_all(tensor, "bitb", split_axis=1, concat_axis=1, tiled=True)
    tensor = contract(tensor, own_gates[1], mix_second).astype(jnp.bfloat16)
    tensor = lax.all_to_all(
        tensor.reshape(2, joint_size, row_count // joint_size, width_k),
        ("bita", "bitb"),
        split_axis=1,
        concat_axis=1,
        tiled=True,
    )
    result = contract(tensor, last_gate, mix_joint)
    amplitudes = lax.psum_scatter(result, "cuts", scatter_dimension=2, tiled=True)
    return amplitudes.reshape(2, 1, 1, joint_size, amplitudes.shape[2], width_k)


def dot(a, b):
    return jnp.dot(a, b, preferred_element_type=F32)


def wide(real, imag):
    return (
        jnp.concatenate([real, imag], axis=1),
        jnp.concatenate([-imag, real], axis=1),
    )


def kernel(
    x_hbm, gates_hbm, last_hbm, m1_hbm, m2_hbm, mj_hbm, out_ref,
    x_ref, gates_ref, last_ref, m1_ref, m2_ref, mj_ref,
    send_a, recv_a, send_b, recv_b, send_c, recv_c, send_d, recv_d,
    load_sem, a_send_sem, a_recv_sem, b_send_sem, b_recv_sem,
    c_send_sem, c_recv_sem, d_send_sem, d_recv_sem,
):
    cut = lax.axis_index("cuts")
    bita = lax.axis_index("bita")
    bitb = lax.axis_index("bitb")
    na, nb = 4, 2
    _, rows, width = x_ref.shape
    fine = out_ref.shape[4]
    y, core = cut // 2, lax.rem(cut, 2)
    at_core = y * 2 + (1 - core)
    at_y = (1 - y) * 2 + core
    to_core = (at_core, bita, bitb)
    to_y = (at_y, bita, bitb)
    to_x = (cut, bita, 1 - bitb)
    to_z = [(cut, lax.rem(bita + d, na), bitb) for d in range(1, na)]

    def load(src, dst, i):
        copy = pltpu.make_async_copy(src, dst, load_sem.at[i])
        copy.start()
        return copy

    load_gates = [load(gates_hbm.at[0, i], gates_ref.at[i], i) for i in (1, 0)]
    load_x = [load(x_hbm.at[0, z, 0, 0], x_ref.at[z], 2 + z) for z in range(2)]
    load_rest = [
        load(src, dst, 4 + i)
        for i, (src, dst) in enumerate((
            (m1_hbm, m1_ref), (m2_hbm, m2_ref), (mj_hbm, mj_ref), (last_hbm, last_ref)
        ))
    ]

    barrier = pltpu.get_barrier_semaphore()
    for device in [to_core, to_y, to_x] + to_z:
        pl.semaphore_signal(barrier, inc=1, device_id=device, device_id_type=MESH)

    for copy in load_gates:
        copy.wait()
    g1 = wide(gates_ref[1, 0], gates_ref[1, 1])
    both = dot(gates_ref[0, 0], g1[0]) + dot(gates_ref[0, 1], g1[1])
    both = both.astype(BF16)
    gate = wide(both[:, :width], both[:, width:])
    for copy in load_x:
        copy.wait()

    chunks = ((0, 2), (1, 3))
    halves = (1 - bitb, bitb)
    part = 2 * fine

    def product(target):
        parts = []
        for z in range(2):
            pieces = []
            for half in halves:
                for chunk in chunks:
                    for u in chunk:
                        start = u * (rows // na) + half * (rows // na // nb) + target * fine
                        pieces.append(x_ref[z, pl.ds(pl.multiple_of(start, 16), fine), :])
            parts.append(jnp.concatenate(pieces, axis=0))
        return dot(parts[0], gate[0]) + dot(parts[1], gate[1])

    def remote(src, dst, send_sem, recv_sem, device):
        return pltpu.make_async_remote_copy(
            src_ref=src, dst_ref=dst, send_sem=send_sem, recv_sem=recv_sem,
            device_id=device, device_id_type=MESH,
        )

    a_copies, b_copies, c_copies, d_copies = [], [], [], []
    for i, target in enumerate(((1 - y) * 2 + (1 - core), y * 2 + (1 - core))):
        send_a[i] = product(target).astype(BF16)
        if i == 0:
            pl.semaphore_wait(barrier, 6)
        copy = remote(send_a.at[i], recv_a.at[i], a_send_sem.at[i], a_recv_sem.at[i], to_core)
        copy.start()
        a_copies.append(copy)

    total = product(at_y)
    a_copies[0].wait_recv()
    for q in range(4):
        rows_q = slice(q * part, (q + 1) * part)
        send_b[q] = (total[rows_q] + recv_a[0, rows_q].astype(F32)).astype(BF16)
        copy = remote(send_b.at[q], recv_b.at[q], b_send_sem.at[q], b_recv_sem.at[q], to_y)
        copy.start()
        b_copies.append(copy)
    total = product(cut)
    a_copies[1].wait_recv()
    total = total + recv_a[1].astype(F32)

    def summed(q):
        b_copies[q].wait_recv()
        return total[q * part:(q + 1) * part] + recv_b[q].astype(F32)

    for copy in load_rest:
        copy.wait()
    low = lax.rem(bita, 2)
    lanes = na * na * fine
    by_fine = fine.bit_length() - 1
    w_id = lax.broadcasted_iota(jnp.int32, (na * nb, lanes), 0)
    lane = lax.broadcasted_iota(jnp.int32, (na * nb, lanes), 1)
    u_id = (((lane >> by_fine) & 1) << 1) | (lane >> (by_fine + 3))
    d_id = (lane >> (by_fine + 1)) & 3
    mixed = [jnp.zeros((na * nb, lanes), F32), jnp.zeros((na * nb, lanes), F32)]
    for b in range(nb):
        first, joint = [], []
        for z in range(2):
            a_part = jnp.zeros((na * nb, lanes), F32)
            for d in range(na):
                a_part = jnp.where(d_id == d, m1_ref[z, lax.rem(bita + d, na), b * 2 + low], a_part)
            j_part = jnp.zeros((na * nb, lanes), F32)
            for u in range(na):
                for w in range(na * nb):
                    j_part = jnp.where((u_id == u) & (w_id == w), mj_ref[z, u * nb + b, w], j_part)
            first.append(a_part)
            joint.append(j_part)
        mixed[0] += first[0] * joint[0] - first[1] * joint[1]
        mixed[1] += first[0] * joint[1] + first[1] * joint[0]

    for h in range(2):
        send_c[h] = summed(h).astype(BF16)
        copy = remote(send_c.at[h], recv_c.at[h], c_send_sem.at[h], c_recv_sem.at[h], to_x)
        copy.start()
        c_copies.append(copy)

    same = (
        lax.broadcasted_iota(jnp.int32, (fine, lanes), 1) & (fine - 1)
    ) == lax.broadcasted_iota(jnp.int32, (fine, lanes), 0)
    spread = jnp.concatenate([
        jnp.where(same, mixed[z][w:w + 1], 0.0) for z in range(2) for w in range(na * nb)
    ], axis=0).astype(BF16)
    last = wide(last_ref[0], last_ref[1])

    for h in range(2):
        own = summed(2 + h)
        own_r, own_i = own[:, :width], own[:, width:]
        c_copies[h].wait_recv()
        other = recv_c[h].astype(F32)
        other_r, other_i = other[:, :width], other[:, width:]
        for v in range(nb):
            kr, ki = m2_ref[0, bitb, v], m2_ref[1, bitb, v]
            pr, pi = m2_ref[0, 1 - bitb, v], m2_ref[1, 1 - bitb, v]
            send_d[h, v] = jnp.concatenate([
                own_r * kr - own_i * ki + other_r * pr - other_i * pi,
                own_r * ki + own_i * kr + other_r * pi + other_i * pr,
            ], axis=1).astype(BF16)
        for d in (2, 1, 3):
            to = lax.rem(bita + d, na)
            copy = remote(
                send_d.at[h, to // 2], recv_d.at[h, na - 1 - d], d_send_sem.at[h, d - 1],
                d_recv_sem.at[h, na - 1 - d], (cut, to, bitb),
            )
            copy.start()
            d_copies.append(copy)

    columns = na * part
    sums = None
    for h in range(2):
        for copy in d_copies[h * (na - 1):(h + 1) * (na - 1)]:
            copy.wait_recv()
        value = jnp.concatenate(
            [send_d[h, bita // 2]] + [recv_d[h, s] for s in range(na - 1)], axis=0
        )
        more = dot(spread[:, h * columns:(h + 1) * columns], value)
        sums = more if sums is None else sums + more
    count = na * nb * fine
    real = (sums[:count, :width] - sums[count:, width:]).astype(BF16)
    imag = (sums[:count, width:] + sums[count:, :width]).astype(BF16)
    result = dot(real, last[0]) + dot(imag, last[1])
    for z in range(2):
        out_ref[z, 0, 0] = result[:, z * width:(z + 1) * width].reshape(na * nb, fine, width)
    for copy in a_copies + b_copies + c_copies + d_copies:
        copy.wait_send()


def by_kernel(slice_tensors, slice_gates, last_gate, mix_first, mix_second, mix_joint):
    rows, width = slice_tensors.shape[4:]
    na, nb, cuts = lax.axis_size("bita"), lax.axis_size("bitb"), lax.axis_size("cuts")
    fine = rows // (na * nb * cuts)
    part = 2 * fine
    hbm = pl.BlockSpec(memory_space=pltpu.MemorySpace.HBM)
    dma = pltpu.SemaphoreType.DMA
    return pl.pallas_call(
        kernel,
        out_shape=jax.ShapeDtypeStruct((2, 1, 1, na * nb, fine, width), F32),
        in_specs=[hbm] * 6,
        out_specs=pl.BlockSpec(memory_space=pltpu.VMEM),
        scratch_shapes=[
            pltpu.VMEM((2, rows, width), BF16),
            pltpu.VMEM(slice_gates.shape[1:], BF16),
            pltpu.VMEM(last_gate.shape, BF16),
            pltpu.SMEM(mix_first.shape, F32),
            pltpu.SMEM(mix_second.shape, F32),
            pltpu.SMEM(mix_joint.shape, F32),
            pltpu.VMEM((2, 4 * part, 2 * width), BF16),
            pltpu.VMEM((2, 4 * part, 2 * width), BF16),
            pltpu.VMEM((4, part, 2 * width), BF16),
            pltpu.VMEM((4, part, 2 * width), BF16),
            pltpu.VMEM((2, part, 2 * width), BF16),
            pltpu.VMEM((2, part, 2 * width), BF16),
            pltpu.VMEM((2, nb, part, 2 * width), BF16),
            pltpu.VMEM((2, na - 1, part, 2 * width), BF16),
            dma((8,)), dma((2,)), dma((2,)), dma((4,)), dma((4,)),
            dma((2,)), dma((2,)), dma((2, na - 1)), dma((2, na - 1)),
        ],
        compiler_params=pltpu.CompilerParams(
            collective_id=0, has_side_effects=True, vmem_limit_bytes=56 * 2**20
        ),
    )(slice_tensors, slice_gates, last_gate, mix_first, mix_second, mix_joint)


def solution(mesh):
    placed = (
        P("cuts", None, "bita", "bitb", None, None),
        P("cuts", None, None, None, None),
        P(),
        P(),
        P(),
        P(),
    )
    pairs = (mesh.shape["cuts"], mesh.shape["bita"], mesh.shape["bitb"]) == (4, 4, 2)
    return jax.shard_map(
        by_kernel if pairs else by_collectives,
        mesh=mesh,
        in_specs=placed,
        out_specs=P(None, "bita", "bitb", None, "cuts", None),
        check_vma=False,
    )
```

```python
import functools

import jax
import jax.numpy as jnp
from jax import lax
from jax.experimental import pallas as pl
from jax.experimental.pallas import tpu as pltpu
from jax.sharding import PartitionSpec as P

MESH = pl.DeviceIdType.MESH
BF16 = jnp.bfloat16
F32 = jnp.float32


def mix_group(values, matrix):
    return jnp.einsum("...csm,cd->...dsm", values, matrix, precision=lax.Precision.HIGHEST)


def contract(tensor, gate_pair, mixing):
    products = jnp.einsum(
        "z...k,wkm->zw...m", tensor, gate_pair, preferred_element_type=jnp.float32
    )
    real_part = products[0, 0] - products[1, 1]
    imag_part = products[0, 1] + products[1, 0]
    out_real = mix_group(real_part, mixing[0]) - mix_group(imag_part, mixing[1])
    out_imag = mix_group(real_part, mixing[1]) + mix_group(imag_part, mixing[0])
    return jnp.stack([out_real, out_imag])


def by_collectives(slice_tensors, slice_gates, last_gate, mix_first, mix_second, mix_joint):
    row_count = slice_tensors.shape[4]
    width_k = slice_tensors.shape[5]
    bita_size = lax.axis_size("bita")
    bitb_size = lax.axis_size("bitb")
    joint_size = bita_size * bitb_size
    own_gates = slice_gates[0]
    tensor = slice_tensors.reshape(2, bita_size, row_count // bita_size, width_k)
    tensor = lax.all_to_all(tensor, "bita", split_axis=1, concat_axis=1, tiled=True)
    tensor = contract(tensor, own_gates[0], mix_first).astype(jnp.bfloat16)
    tensor = tensor.reshape(2, bitb_size, row_count // bitb_size, width_k)
    tensor = lax.all_to_all(tensor, "bitb", split_axis=1, concat_axis=1, tiled=True)
    tensor = contract(tensor, own_gates[1], mix_second).astype(jnp.bfloat16)
    tensor = lax.all_to_all(
        tensor.reshape(2, joint_size, row_count // joint_size, width_k),
        ("bita", "bitb"),
        split_axis=1,
        concat_axis=1,
        tiled=True,
    )
    result = contract(tensor, last_gate, mix_joint)
    amplitudes = lax.psum_scatter(result, "cuts", scatter_dimension=2, tiled=True)
    return amplitudes.reshape(2, 1, 1, joint_size, amplitudes.shape[2], width_k)


def dot(a, b):
    return jnp.dot(a, b, preferred_element_type=F32)


def wide(real, imag):
    return (
        jnp.concatenate([real, imag], axis=1),
        jnp.concatenate([-imag, real], axis=1),
    )


def kernel(
    x_hbm, gates_hbm, last_hbm, m1_hbm, m2_hbm, mj_hbm, out_ref,
    x_ref, gates_ref, last_ref, m1_ref, m2_ref, mj_ref,
    send_a, recv_a, send_b, recv_b, send_c, recv_c, send_d, recv_d,
    load_sem, a_send_sem, a_recv_sem, b_send_sem, b_recv_sem,
    c_send_sem, c_recv_sem, d_send_sem, d_recv_sem,
):
    cut = lax.axis_index("cuts")
    bita = lax.axis_index("bita")
    bitb = lax.axis_index("bitb")
    na, nb = 4, 2
    _, rows, width = x_ref.shape
    fine = out_ref.shape[4]
    y, core = cut // 2, lax.rem(cut, 2)
    at_core = y * 2 + (1 - core)
    at_y = (1 - y) * 2 + core
    to_core = (at_core, bita, bitb)
    to_y = (at_y, bita, bitb)
    to_x = (cut, bita, 1 - bitb)
    to_z = [(cut, lax.rem(bita + d, na), bitb) for d in range(1, na)]

    def load(src, dst, i):
        copy = pltpu.make_async_copy(src, dst, load_sem.at[i])
        copy.start()
        return copy

    load_gates = [load(gates_hbm.at[0, i], gates_ref.at[i], i) for i in (1, 0)]
    load_x = [load(x_hbm.at[0, z, 0, 0], x_ref.at[z], 2 + z) for z in range(2)]
    load_rest = [
        load(src, dst, 4 + i)
        for i, (src, dst) in enumerate((
            (m1_hbm, m1_ref), (m2_hbm, m2_ref), (mj_hbm, mj_ref), (last_hbm, last_ref)
        ))
    ]

    barrier = pltpu.get_barrier_semaphore()
    for device in [to_core, to_y, to_x] + to_z:
        pl.semaphore_signal(barrier, inc=1, device_id=device, device_id_type=MESH)

    for copy in load_gates:
        copy.wait()
    g1 = wide(gates_ref[1, 0], gates_ref[1, 1])
    both = dot(gates_ref[0, 0], g1[0]) + dot(gates_ref[0, 1], g1[1])
    both = both.astype(BF16)
    gate = wide(both[:, :width], both[:, width:])
    for copy in load_x:
        copy.wait()

    halves = (1 - bitb, bitb)
    part = fine

    def product(target):
        parts = []
        for z in range(2):
            pieces = []
            for half in halves:
                for u in range(na):
                    start = u * (rows // na) + half * (rows // na // nb) + target * fine
                    pieces.append(x_ref[z, pl.ds(pl.multiple_of(start, 16), fine), :])
            parts.append(jnp.concatenate(pieces, axis=0))
        return dot(parts[0], gate[0]) + dot(parts[1], gate[1])

    def remote(src, dst, send_sem, recv_sem, device):
        return pltpu.make_async_remote_copy(
            src_ref=src, dst_ref=dst, send_sem=send_sem, recv_sem=recv_sem,
            device_id=device, device_id_type=MESH,
        )

    a_copies, b_copies, c_copies, d_copies = [], {}, [], []
    for i, target in enumerate(((1 - y) * 2 + (1 - core), y * 2 + (1 - core))):
        send_a[i] = product(target).astype(BF16)
        if i == 0:
            pl.semaphore_wait(barrier, 6)
        copy = remote(send_a.at[i], recv_a.at[i], a_send_sem.at[i], a_recv_sem.at[i], to_core)
        copy.start()
        a_copies.append(copy)

    total = product(at_y)
    a_copies[0].wait_recv()
    order = (0, 1, 2, 4, 3, 5, 6, 7)
    for q in order:
        rows_q = slice(q * part, (q + 1) * part)
        send_b[q] = (total[rows_q] + recv_a[0, rows_q].astype(F32)).astype(BF16)
        copy = remote(send_b.at[q], recv_b.at[q], b_send_sem.at[q], b_recv_sem.at[q], to_y)
        copy.start()
        b_copies[q] = copy
    total = product(cut)
    a_copies[1].wait_recv()
    total = total + recv_a[1].astype(F32)

    def summed(q):
        b_copies[q].wait_recv()
        return total[q * part:(q + 1) * part] + recv_b[q].astype(F32)

    for copy in load_rest:
        copy.wait()
    low = lax.rem(bita, 2)
    lanes = na * na * fine
    by_fine = fine.bit_length() - 1
    w_id = lax.broadcasted_iota(jnp.int32, (na * nb, lanes), 0)
    lane = lax.broadcasted_iota(jnp.int32, (na * nb, lanes), 1)
    u_id = lane >> (by_fine + 2)
    d_id = (lane >> by_fine) & 3
    mixed = [jnp.zeros((na * nb, lanes), F32), jnp.zeros((na * nb, lanes), F32)]
    for b in range(nb):
        first, joint = [], []
        for z in range(2):
            a_part = jnp.zeros((na * nb, lanes), F32)
            for d in range(na):
                a_part = jnp.where(d_id == d, m1_ref[z, lax.rem(bita + d, na), b * 2 + low], a_part)
            j_part = jnp.zeros((na * nb, lanes), F32)
            for u in range(na):
                for w in range(na * nb):
                    j_part = jnp.where((u_id == u) & (w_id == w), mj_ref[z, u * nb + b, w], j_part)
            first.append(a_part)
            joint.append(j_part)
        mixed[0] += first[0] * joint[0] - first[1] * joint[1]
        mixed[1] += first[0] * joint[1] + first[1] * joint[0]

    for h in range(na):
        send_c[h] = summed(h).astype(BF16)
        copy = remote(send_c.at[h], recv_c.at[h], c_send_sem.at[h], c_recv_sem.at[h], to_x)
        copy.start()
        c_copies.append(copy)

    same = (
        lax.broadcasted_iota(jnp.int32, (fine, lanes), 1) & (fine - 1)
    ) == lax.broadcasted_iota(jnp.int32, (fine, lanes), 0)
    spread = jnp.concatenate([
        jnp.where(same, mixed[z][w:w + 1], 0.0) for z in range(2) for w in range(na * nb)
    ], axis=0).astype(BF16)
    last = wide(last_ref[0], last_ref[1])

    for h in range(na):
        own = summed(na + h)
        own_r, own_i = own[:, :width], own[:, width:]
        c_copies[h].wait_recv()
        other = recv_c[h].astype(F32)
        other_r, other_i = other[:, :width], other[:, width:]
        for v in range(nb):
            kr, ki = m2_ref[0, bitb, v], m2_ref[1, bitb, v]
            pr, pi = m2_ref[0, 1 - bitb, v], m2_ref[1, 1 - bitb, v]
            send_d[h, v] = jnp.concatenate([
                own_r * kr - own_i * ki + other_r * pr - other_i * pi,
                own_r * ki + own_i * kr + other_r * pi + other_i * pr,
            ], axis=1).astype(BF16)
        for d in (2, 1, 3):
            to = lax.rem(bita + d, na)
            copy = remote(
                send_d.at[h, to // 2], recv_d.at[h, na - 1 - d], d_send_sem.at[h, d - 1],
                d_recv_sem.at[h, na - 1 - d], (cut, to, bitb),
            )
            copy.start()
            d_copies.append(copy)

    columns = 2 * na * part
    sums = None
    for g in range(2):
        pieces = []
        for h in (2 * g, 2 * g + 1):
            for copy in d_copies[h * (na - 1):(h + 1) * (na - 1)]:
                copy.wait_recv()
            pieces += [send_d[h, bita // 2]] + [recv_d[h, s] for s in range(na - 1)]
        value = jnp.concatenate(pieces, axis=0)
        more = dot(spread[:, g * columns:(g + 1) * columns], value)
        sums = more if sums is None else sums + more
    count = na * nb * fine
    real = (sums[:count, :width] - sums[count:, width:]).astype(BF16)
    imag = (sums[:count, width:] + sums[count:, :width]).astype(BF16)
    result = dot(real, last[0]) + dot(imag, last[1])
    for z in range(2):
        out_ref[z, 0, 0] = result[:, z * width:(z + 1) * width].reshape(na * nb, fine, width)
    for copy in a_copies + [b_copies[q] for q in order] + c_copies + d_copies:
        copy.wait_send()


def by_kernel(slice_tensors, slice_gates, last_gate, mix_first, mix_second, mix_joint):
    rows, width = slice_tensors.shape[4:]
    na, nb, cuts = lax.axis_size("bita"), lax.axis_size("bitb"), lax.axis_size("cuts")
    fine = rows // (na * nb * cuts)
    part = fine
    hbm = pl.BlockSpec(memory_space=pltpu.MemorySpace.HBM)
    dma = pltpu.SemaphoreType.DMA
    return pl.pallas_call(
        kernel,
        out_shape=pltpu.VMEM((2, 1, 1, na * nb, fine, width), F32),
        in_specs=[hbm] * 6,
        out_specs=pl.BlockSpec(memory_space=pltpu.VMEM),
        scratch_shapes=[
            pltpu.VMEM((2, rows, width), BF16),
            pltpu.VMEM(slice_gates.shape[1:], BF16),
            pltpu.VMEM(last_gate.shape, BF16),
            pltpu.SMEM(mix_first.shape, F32),
            pltpu.SMEM(mix_second.shape, F32),
            pltpu.SMEM(mix_joint.shape, F32),
            pltpu.VMEM((2, 8 * part, 2 * width), BF16),
            pltpu.VMEM((2, 8 * part, 2 * width), BF16),
            pltpu.VMEM((8, part, 2 * width), BF16),
            pltpu.VMEM((8, part, 2 * width), BF16),
            pltpu.VMEM((na, part, 2 * width), BF16),
            pltpu.VMEM((na, part, 2 * width), BF16),
            pltpu.VMEM((na, nb, part, 2 * width), BF16),
            pltpu.VMEM((na, na - 1, part, 2 * width), BF16),
            dma((8,)), dma((2,)), dma((2,)), dma((8,)), dma((8,)),
            dma((na,)), dma((na,)), dma((na, na - 1)), dma((na, na - 1)),
        ],
        compiler_params=pltpu.CompilerParams(
            collective_id=0, has_side_effects=True, vmem_limit_bytes=56 * 2**20
        ),
    )(slice_tensors, slice_gates, last_gate, mix_first, mix_second, mix_joint)


def solution(mesh):
    placed = (
        P("cuts", None, "bita", "bitb", None, None),
        P("cuts", None, None, None, None),
        P(),
        P(),
        P(),
        P(),
    )
    pairs = (mesh.shape["cuts"], mesh.shape["bita"], mesh.shape["bitb"]) == (4, 4, 2)
    return jax.shard_map(
        by_kernel if pairs else by_collectives,
        mesh=mesh,
        in_specs=placed,
        out_specs=P(None, "bita", "bitb", None, "cuts", None),
        check_vma=False,
    )
```

```python
import functools

import jax
import jax.numpy as jnp
from jax import lax
from jax.experimental import pallas as pl
from jax.experimental.pallas import tpu as pltpu
from jax.sharding import PartitionSpec as P

MESH = pl.DeviceIdType.MESH
BF16 = jnp.bfloat16
F32 = jnp.float32


def mix_group(values, matrix):
    return jnp.einsum("...csm,cd->...dsm", values, matrix, precision=lax.Precision.HIGHEST)


def contract(tensor, gate_pair, mixing):
    products = jnp.einsum(
        "z...k,wkm->zw...m", tensor, gate_pair, preferred_element_type=jnp.float32
    )
    real_part = products[0, 0] - products[1, 1]
    imag_part = products[0, 1] + products[1, 0]
    out_real = mix_group(real_part, mixing[0]) - mix_group(imag_part, mixing[1])
    out_imag = mix_group(real_part, mixing[1]) + mix_group(imag_part, mixing[0])
    return jnp.stack([out_real, out_imag])


def by_collectives(slice_tensors, slice_gates, last_gate, mix_first, mix_second, mix_joint):
    row_count = slice_tensors.shape[4]
    width_k = slice_tensors.shape[5]
    bita_size = lax.axis_size("bita")
    bitb_size = lax.axis_size("bitb")
    joint_size = bita_size * bitb_size
    own_gates = slice_gates[0]
    tensor = slice_tensors.reshape(2, bita_size, row_count // bita_size, width_k)
    tensor = lax.all_to_all(tensor, "bita", split_axis=1, concat_axis=1, tiled=True)
    tensor = contract(tensor, own_gates[0], mix_first).astype(jnp.bfloat16)
    tensor = tensor.reshape(2, bitb_size, row_count // bitb_size, width_k)
    tensor = lax.all_to_all(tensor, "bitb", split_axis=1, concat_axis=1, tiled=True)
    tensor = contract(tensor, own_gates[1], mix_second).astype(jnp.bfloat16)
    tensor = lax.all_to_all(
        tensor.reshape(2, joint_size, row_count // joint_size, width_k),
        ("bita", "bitb"),
        split_axis=1,
        concat_axis=1,
        tiled=True,
    )
    result = contract(tensor, last_gate, mix_joint)
    amplitudes = lax.psum_scatter(result, "cuts", scatter_dimension=2, tiled=True)
    return amplitudes.reshape(2, 1, 1, joint_size, amplitudes.shape[2], width_k)


def dot(a, b):
    return jnp.dot(a, b, preferred_element_type=F32)


def wide(real, imag):
    return (
        jnp.concatenate([real, imag], axis=1),
        jnp.concatenate([-imag, real], axis=1),
    )


def kernel(
    x_hbm, gates_hbm, last_hbm, m1_hbm, m2_hbm, mj_hbm, out_ref,
    x_ref, gates_ref, last_ref, m1_ref, m2_ref, mj_ref,
    send_a, recv_a, send_b, recv_b, send_c, recv_c, send_d, recv_d,
    load_sem, a_send_sem, a_recv_sem, b_send_sem, b_recv_sem,
    c_send_sem, c_recv_sem, d_send_sem, d_recv_sem,
):
    cut = lax.axis_index("cuts")
    bita = lax.axis_index("bita")
    bitb = lax.axis_index("bitb")
    na, nb = 4, 2
    _, rows, width = x_ref.shape
    fine = out_ref.shape[4]
    y, core = cut // 2, lax.rem(cut, 2)
    at_core = y * 2 + (1 - core)
    at_y = (1 - y) * 2 + core
    to_core = (at_core, bita, bitb)
    to_y = (at_y, bita, bitb)
    to_x = (cut, bita, 1 - bitb)
    at_z = [bita, bita + 1 - 2 * lax.rem(bita, 2), lax.rem(bita + 2, na), na - 1 - bita]
    to_z = [(cut, at, bitb) for at in at_z[1:]]

    def load(src, dst, i):
        copy = pltpu.make_async_copy(src, dst, load_sem.at[i])
        copy.start()
        return copy

    load_gates = [load(gates_hbm.at[0, i], gates_ref.at[i], i) for i in (1, 0)]
    load_x = [load(x_hbm.at[0, z, 0, 0], x_ref.at[z], 2 + z) for z in range(2)]
    load_rest = [
        load(src, dst, 4 + i)
        for i, (src, dst) in enumerate((
            (m1_hbm, m1_ref), (m2_hbm, m2_ref), (mj_hbm, mj_ref), (last_hbm, last_ref)
        ))
    ]

    barrier = pltpu.get_barrier_semaphore()
    for device in [to_core, to_y, to_x] + to_z:
        pl.semaphore_signal(barrier, inc=1, device_id=device, device_id_type=MESH)

    for copy in load_gates:
        copy.wait()
    g1 = wide(gates_ref[1, 0], gates_ref[1, 1])
    both = dot(gates_ref[0, 0], g1[0]) + dot(gates_ref[0, 1], g1[1])
    both = both.astype(BF16)
    gate = wide(both[:, :width], both[:, width:])
    for copy in load_x:
        copy.wait()

    halves = (1 - bitb, bitb)
    part = fine

    def product(target):
        parts = []
        for z in range(2):
            pieces = []
            for half in halves:
                for u in range(na):
                    start = u * (rows // na) + half * (rows // na // nb) + target * fine
                    pieces.append(x_ref[z, pl.ds(pl.multiple_of(start, 16), fine), :])
            parts.append(jnp.concatenate(pieces, axis=0))
        return dot(parts[0], gate[0]) + dot(parts[1], gate[1])

    def remote(src, dst, send_sem, recv_sem, device):
        return pltpu.make_async_remote_copy(
            src_ref=src, dst_ref=dst, send_sem=send_sem, recv_sem=recv_sem,
            device_id=device, device_id_type=MESH,
        )

    a_copies, b_copies, c_copies, d_copies = [], {}, [], {}
    for i, target in enumerate(((1 - y) * 2 + (1 - core), y * 2 + (1 - core))):
        send_a[i] = product(target).astype(BF16)
        if i == 0:
            pl.semaphore_wait(barrier, 6)
        for half in range(2):
            rows_half = pl.ds(half * na * part, na * part)
            copy = remote(
                send_a.at[i, rows_half], recv_a.at[i, rows_half],
                a_send_sem.at[i, half], a_recv_sem.at[i, half], to_core,
            )
            copy.start()
            a_copies.append(copy)

    total = product(at_y)
    a_copies[0].wait_recv()
    order = (0, 1, 2, 3, 4, 5, 6, 7)
    for q in order:
        if q == na:
            a_copies[1].wait_recv()
        rows_q = slice(q * part, (q + 1) * part)
        send_b[q] = (total[rows_q] + recv_a[0, rows_q].astype(F32)).astype(BF16)
        copy = remote(send_b.at[q], recv_b.at[q], b_send_sem.at[q], b_recv_sem.at[q], to_y)
        copy.start()
        b_copies[q] = copy
    total = product(cut)
    a_copies[2].wait_recv()
    a_copies[3].wait_recv()
    total = total + recv_a[1].astype(F32)

    def summed(q):
        b_copies[q].wait_recv()
        return total[q * part:(q + 1) * part] + recv_b[q].astype(F32)

    for copy in load_rest:
        copy.wait()
    low = lax.rem(bita, 2)
    lanes = na * na * fine
    by_fine = fine.bit_length() - 1
    w_id = lax.broadcasted_iota(jnp.int32, (na * nb, lanes), 0)
    lane = lax.broadcasted_iota(jnp.int32, (na * nb, lanes), 1)
    u_id = lane >> (by_fine + 2)
    d_id = (lane >> by_fine) & 3
    mixed = [jnp.zeros((na * nb, lanes), F32), jnp.zeros((na * nb, lanes), F32)]
    for b in range(nb):
        first, joint = [], []
        for z in range(2):
            a_part = jnp.zeros((na * nb, lanes), F32)
            for d in range(na):
                a_part = jnp.where(d_id == d, m1_ref[z, at_z[d], b * 2 + low], a_part)
            j_part = jnp.zeros((na * nb, lanes), F32)
            for u in range(na):
                for w in range(na * nb):
                    j_part = jnp.where((u_id == u) & (w_id == w), mj_ref[z, u * nb + b, w], j_part)
            first.append(a_part)
            joint.append(j_part)
        mixed[0] += first[0] * joint[0] - first[1] * joint[1]
        mixed[1] += first[0] * joint[1] + first[1] * joint[0]

    for h in range(na):
        send_c[h] = summed(h).astype(BF16)
        copy = remote(send_c.at[h], recv_c.at[h], c_send_sem.at[h], c_recv_sem.at[h], to_x)
        copy.start()
        c_copies.append(copy)

    same = (
        lax.broadcasted_iota(jnp.int32, (fine, lanes), 1) & (fine - 1)
    ) == lax.broadcasted_iota(jnp.int32, (fine, lanes), 0)
    spread = jnp.concatenate([
        jnp.where(same, mixed[z][w:w + 1], 0.0) for z in range(2) for w in range(na * nb)
    ], axis=0).astype(BF16)
    last = wide(last_ref[0], last_ref[1])

    def d_start(src, h, slot, d):
        copy = remote(
            src, recv_d.at[h, slot - 1], d_send_sem.at[h, slot - 1],
            d_recv_sem.at[h, slot - 1], to_z[d - 1],
        )
        copy.start()
        d_copies[h, slot] = copy

    for h in range(na):
        own = summed(na + h)
        own_r, own_i = own[:, :width], own[:, width:]
        c_copies[h].wait_recv()
        other = recv_c[h].astype(F32)
        other_r, other_i = other[:, :width], other[:, width:]
        for v in range(nb):
            kr, ki = m2_ref[0, bitb, v], m2_ref[1, bitb, v]
            pr, pi = m2_ref[0, 1 - bitb, v], m2_ref[1, 1 - bitb, v]
            send_d[h, v] = jnp.concatenate([
                own_r * kr - own_i * ki + other_r * pr - other_i * pi,
                own_r * ki + own_i * kr + other_r * pi + other_i * pr,
            ], axis=1).astype(BF16)
        for d in ((2, 1) if h < 2 else (3, 2, 1)):
            d_start(send_d.at[h, at_z[d] // 2], h, d, d)
        if h >= 2:
            d_copies[h - 2, 2].wait_recv()
            d_start(recv_d.at[h - 2, 1], h - 2, 3, 1)

    columns = 2 * na * part
    sums = None
    for g in range(2):
        pieces = []
        for h in (2 * g, 2 * g + 1):
            for slot in range(1, na):
                if h >= 2 or slot != 2:
                    d_copies[h, slot].wait_recv()
            pieces += [send_d[h, bita // 2]] + [recv_d[h, s] for s in range(na - 1)]
        value = jnp.concatenate(pieces, axis=0)
        more = dot(spread[:, g * columns:(g + 1) * columns], value)
        sums = more if sums is None else sums + more
    count = na * nb * fine
    real = (sums[:count, :width] - sums[count:, width:]).astype(BF16)
    imag = (sums[:count, width:] + sums[count:, :width]).astype(BF16)
    result = dot(real, last[0]) + dot(imag, last[1])
    for z in range(2):
        out_ref[z, 0, 0] = result[:, z * width:(z + 1) * width].reshape(na * nb, fine, width)
    for copy in a_copies + list(b_copies.values()) + c_copies + list(d_copies.values()):
        copy.wait_send()


def by_kernel(slice_tensors, slice_gates, last_gate, mix_first, mix_second, mix_joint):
    rows, width = slice_tensors.shape[4:]
    na, nb, cuts = lax.axis_size("bita"), lax.axis_size("bitb"), lax.axis_size("cuts")
    fine = rows // (na * nb * cuts)
    part = fine
    hbm = pl.BlockSpec(memory_space=pltpu.MemorySpace.HBM)
    dma = pltpu.SemaphoreType.DMA
    return pl.pallas_call(
        kernel,
        out_shape=pltpu.VMEM((2, 1, 1, na * nb, fine, width), F32),
        in_specs=[hbm] * 6,
        out_specs=pl.BlockSpec(memory_space=pltpu.VMEM),
        scratch_shapes=[
            pltpu.VMEM((2, rows, width), BF16),
            pltpu.VMEM(slice_gates.shape[1:], BF16),
            pltpu.VMEM(last_gate.shape, BF16),
            pltpu.SMEM(mix_first.shape, F32),
            pltpu.SMEM(mix_second.shape, F32),
            pltpu.SMEM(mix_joint.shape, F32),
            pltpu.VMEM((2, 8 * part, 2 * width), BF16),
            pltpu.VMEM((2, 8 * part, 2 * width), BF16),
            pltpu.VMEM((8, part, 2 * width), BF16),
            pltpu.VMEM((8, part, 2 * width), BF16),
            pltpu.VMEM((na, part, 2 * width), BF16),
            pltpu.VMEM((na, part, 2 * width), BF16),
            pltpu.VMEM((na, nb, part, 2 * width), BF16),
            pltpu.VMEM((na, na - 1, part, 2 * width), BF16),
            dma((8,)), dma((2, 2)), dma((2, 2)), dma((8,)), dma((8,)),
            dma((na,)), dma((na,)), dma((na, na - 1)), dma((na, na - 1)),
        ],
        compiler_params=pltpu.CompilerParams(
            collective_id=0, has_side_effects=True, vmem_limit_bytes=56 * 2**20
        ),
    )(slice_tensors, slice_gates, last_gate, mix_first, mix_second, mix_joint)


def solution(mesh):
    placed = (
        P("cuts", None, "bita", "bitb", None, None),
        P("cuts", None, None, None, None),
        P(),
        P(),
        P(),
        P(),
    )
    pairs = (mesh.shape["cuts"], mesh.shape["bita"], mesh.shape["bitb"]) == (4, 4, 2)
    return jax.shard_map(
        by_kernel if pairs else by_collectives,
        mesh=mesh,
        in_specs=placed,
        out_specs=P(None, "bita", "bitb", None, "cuts", None),
        check_vma=False,
    )
```

```python
import functools

import jax
import jax.numpy as jnp
from jax import lax
from jax.experimental import pallas as pl
from jax.experimental.pallas import tpu as pltpu
from jax.sharding import PartitionSpec as P

MESH = pl.DeviceIdType.MESH
BF16 = jnp.bfloat16
F32 = jnp.float32


def mix_group(values, matrix):
    return jnp.einsum("...csm,cd->...dsm", values, matrix, precision=lax.Precision.HIGHEST)


def contract(tensor, gate_pair, mixing):
    products = jnp.einsum(
        "z...k,wkm->zw...m", tensor, gate_pair, preferred_element_type=jnp.float32
    )
    real_part = products[0, 0] - products[1, 1]
    imag_part = products[0, 1] + products[1, 0]
    out_real = mix_group(real_part, mixing[0]) - mix_group(imag_part, mixing[1])
    out_imag = mix_group(real_part, mixing[1]) + mix_group(imag_part, mixing[0])
    return jnp.stack([out_real, out_imag])


def by_collectives(slice_tensors, slice_gates, last_gate, mix_first, mix_second, mix_joint):
    row_count = slice_tensors.shape[4]
    width_k = slice_tensors.shape[5]
    bita_size = lax.axis_size("bita")
    bitb_size = lax.axis_size("bitb")
    joint_size = bita_size * bitb_size
    own_gates = slice_gates[0]
    tensor = slice_tensors.reshape(2, bita_size, row_count // bita_size, width_k)
    tensor = lax.all_to_all(tensor, "bita", split_axis=1, concat_axis=1, tiled=True)
    tensor = contract(tensor, own_gates[0], mix_first).astype(jnp.bfloat16)
    tensor = tensor.reshape(2, bitb_size, row_count // bitb_size, width_k)
    tensor = lax.all_to_all(tensor, "bitb", split_axis=1, concat_axis=1, tiled=True)
    tensor = contract(tensor, own_gates[1], mix_second).astype(jnp.bfloat16)
    tensor = lax.all_to_all(
        tensor.reshape(2, joint_size, row_count // joint_size, width_k),
        ("bita", "bitb"),
        split_axis=1,
        concat_axis=1,
        tiled=True,
    )
    result = contract(tensor, last_gate, mix_joint)
    amplitudes = lax.psum_scatter(result, "cuts", scatter_dimension=2, tiled=True)
    return amplitudes.reshape(2, 1, 1, joint_size, amplitudes.shape[2], width_k)


def dot(a, b):
    return jnp.dot(a, b, preferred_element_type=F32)


def wide(real, imag):
    return (
        jnp.concatenate([real, imag], axis=1),
        jnp.concatenate([-imag, real], axis=1),
    )


def kernel(
    x_hbm, gates_hbm, last_hbm, m1_hbm, m2_hbm, mj_hbm, out_ref,
    x_ref, gates_ref, last_ref, m1_ref, m2_ref, mj_ref,
    send_a, recv_a, send_b, recv_b, send_c, recv_c, send_d, recv_d,
    load_sem, a_send_sem, a_recv_sem, b_send_sem, b_recv_sem,
    c_send_sem, c_recv_sem, d_send_sem, d_recv_sem,
):
    cut = lax.axis_index("cuts")
    bita = lax.axis_index("bita")
    bitb = lax.axis_index("bitb")
    na, nb = 4, 2
    _, rows, width = x_ref.shape
    fine = out_ref.shape[4]
    y, core = cut // 2, lax.rem(cut, 2)
    at_core = y * 2 + (1 - core)
    at_y = (1 - y) * 2 + core
    to_core = (at_core, bita, bitb)
    to_y = (at_y, bita, bitb)
    to_x = (cut, bita, 1 - bitb)
    at_z = [bita, bita + 1 - 2 * lax.rem(bita, 2), lax.rem(bita + 2, na), na - 1 - bita]
    to_z = [(cut, at, bitb) for at in at_z[1:]]

    def load(src, dst, i):
        copy = pltpu.make_async_copy(src, dst, load_sem.at[i])
        copy.start()
        return copy

    load_gates = [load(gates_hbm.at[0, i], gates_ref.at[i], i) for i in (1, 0)]
    load_x = [load(x_hbm.at[0, z, 0, 0], x_ref.at[z], 2 + z) for z in range(2)]
    load_rest = [
        load(src, dst, 4 + i)
        for i, (src, dst) in enumerate((
            (m1_hbm, m1_ref), (m2_hbm, m2_ref), (mj_hbm, mj_ref), (last_hbm, last_ref)
        ))
    ]

    barrier = pltpu.get_barrier_semaphore()
    for device in [to_core, to_y, to_x] + to_z:
        pl.semaphore_signal(barrier, inc=1, device_id=device, device_id_type=MESH)

    for copy in load_gates:
        copy.wait()
    g1 = wide(gates_ref[1, 0], gates_ref[1, 1])
    both = dot(gates_ref[0, 0], g1[0]) + dot(gates_ref[0, 1], g1[1])
    both = both.astype(BF16)
    gate = wide(both[:, :width], both[:, width:])
    for copy in load_x:
        copy.wait()

    halves = (1 - bitb, bitb)
    part = fine

    def product(target):
        parts = []
        for z in range(2):
            pieces = []
            for half in halves:
                for u in range(na):
                    start = u * (rows // na) + half * (rows // na // nb) + target * fine
                    pieces.append(x_ref[z, pl.ds(pl.multiple_of(start, 16), fine), :])
            parts.append(jnp.concatenate(pieces, axis=0))
        return dot(parts[0], gate[0]) + dot(parts[1], gate[1])

    def remote(src, dst, send_sem, recv_sem, device):
        return pltpu.make_async_remote_copy(
            src_ref=src, dst_ref=dst, send_sem=send_sem, recv_sem=recv_sem,
            device_id=device, device_id_type=MESH,
        )

    a_copies, b_copies, c_copies, d_copies = [], {}, [], {}
    for i, target in enumerate(((1 - y) * 2 + (1 - core), y * 2 + (1 - core))):
        send_a[i] = product(target).astype(BF16)
        if i == 0:
            pl.semaphore_wait(barrier, 6)
        for half in range(2):
            rows_half = pl.ds(half * na * part, na * part)
            copy = remote(
                send_a.at[i, rows_half], recv_a.at[i, rows_half],
                a_send_sem.at[i, half], a_recv_sem.at[i, half], to_core,
            )
            copy.start()
            a_copies.append(copy)

    total = product(at_y)
    a_copies[0].wait_recv()
    order = (0, 1, 2, 3, 4, 5, 6, 7)
    for q in order:
        if q == na:
            a_copies[1].wait_recv()
        rows_q = slice(q * part, (q + 1) * part)
        send_b[q] = (total[rows_q] + recv_a[0, rows_q].astype(F32)).astype(BF16)
        copy = remote(send_b.at[q], recv_b.at[q], b_send_sem.at[q], b_recv_sem.at[q], to_y)
        copy.start()
        b_copies[q] = copy
    total = product(cut)
    a_copies[2].wait_recv()
    a_copies[3].wait_recv()
    total = total + recv_a[1].astype(F32)

    def summed(q):
        b_copies[q].wait_recv()
        return total[q * part:(q + 1) * part] + recv_b[q].astype(F32)

    for copy in load_rest:
        copy.wait()
    low = lax.rem(bita, 2)
    lanes = na * na * fine
    by_fine = fine.bit_length() - 1
    w_id = lax.broadcasted_iota(jnp.int32, (na * nb, lanes), 0)
    lane = lax.broadcasted_iota(jnp.int32, (na * nb, lanes), 1)
    u_id = lane >> (by_fine + 2)
    d_id = (lane >> by_fine) & 3
    mixed = [jnp.zeros((na * nb, lanes), F32), jnp.zeros((na * nb, lanes), F32)]
    for b in range(nb):
        first, joint = [], []
        for z in range(2):
            a_part = jnp.zeros((na * nb, lanes), F32)
            for d in range(na):
                a_part = jnp.where(d_id == d, m1_ref[z, at_z[d], b * 2 + low], a_part)
            j_part = jnp.zeros((na * nb, lanes), F32)
            for u in range(na):
                for w in range(na * nb):
                    j_part = jnp.where((u_id == u) & (w_id == w), mj_ref[z, u * nb + b, w], j_part)
            first.append(a_part)
            joint.append(j_part)
        mixed[0] += first[0] * joint[0] - first[1] * joint[1]
        mixed[1] += first[0] * joint[1] + first[1] * joint[0]

    for h in range(na):
        send_c[h] = summed(h).astype(BF16)
        copy = remote(send_c.at[h], recv_c.at[h], c_send_sem.at[h], c_recv_sem.at[h], to_x)
        copy.start()
        c_copies.append(copy)

    same = (
        lax.broadcasted_iota(jnp.int32, (fine, lanes), 1) & (fine - 1)
    ) == lax.broadcasted_iota(jnp.int32, (fine, lanes), 0)
    spread = jnp.concatenate([
        jnp.where(same, mixed[z][w:w + 1], 0.0) for z in range(2) for w in range(na * nb)
    ], axis=0).astype(BF16)
    last = wide(last_ref[0], last_ref[1])

    def d_start(src, h, slot, d):
        copy = remote(
            src, recv_d.at[h, slot - 1], d_send_sem.at[h, slot - 1],
            d_recv_sem.at[h, slot - 1], to_z[d - 1],
        )
        copy.start()
        d_copies[h, slot] = copy

    for h in range(na):
        own = summed(na + h)
        own_r, own_i = own[:, :width], own[:, width:]
        c_copies[h].wait_recv()
        other = recv_c[h].astype(F32)
        other_r, other_i = other[:, :width], other[:, width:]
        for v in range(nb):
            kr, ki = m2_ref[0, bitb, v], m2_ref[1, bitb, v]
            pr, pi = m2_ref[0, 1 - bitb, v], m2_ref[1, 1 - bitb, v]
            send_d[h, v] = jnp.concatenate([
                own_r * kr - own_i * ki + other_r * pr - other_i * pi,
                own_r * ki + own_i * kr + other_r * pi + other_i * pr,
            ], axis=1).astype(BF16)
        for d in ((2, 1) if h < 2 else (3, 2, 1)):
            d_start(send_d.at[h, at_z[d] // 2], h, d, d)
    for h in range(2):
        d_copies[h, 2].wait_recv()
        d_start(recv_d.at[h, 1], h, 3, 1)

    columns = 2 * na * part
    sums = None
    for g in (1, 0):
        pieces = []
        for h in (2 * g, 2 * g + 1):
            for slot in range(1, na):
                if h >= 2 or slot != 2:
                    d_copies[h, slot].wait_recv()
            pieces += [send_d[h, bita // 2]] + [recv_d[h, s] for s in range(na - 1)]
        value = jnp.concatenate(pieces, axis=0)
        more = dot(spread[:, g * columns:(g + 1) * columns], value)
        sums = more if sums is None else sums + more
    count = na * nb * fine
    real = (sums[:count, :width] - sums[count:, width:]).astype(BF16)
    imag = (sums[:count, width:] + sums[count:, :width]).astype(BF16)
    result = dot(real, last[0]) + dot(imag, last[1])
    for z in range(2):
        out_ref[z, 0, 0] = result[:, z * width:(z + 1) * width].reshape(na * nb, fine, width)
    for copy in a_copies + list(b_copies.values()) + c_copies + list(d_copies.values()):
        copy.wait_send()


def by_kernel(slice_tensors, slice_gates, last_gate, mix_first, mix_second, mix_joint):
    rows, width = slice_tensors.shape[4:]
    na, nb, cuts = lax.axis_size("bita"), lax.axis_size("bitb"), lax.axis_size("cuts")
    fine = rows // (na * nb * cuts)
    part = fine
    hbm = pl.BlockSpec(memory_space=pltpu.MemorySpace.HBM)
    dma = pltpu.SemaphoreType.DMA
    return pl.pallas_call(
        kernel,
        out_shape=pltpu.VMEM((2, 1, 1, na * nb, fine, width), F32),
        in_specs=[hbm] * 6,
        out_specs=pl.BlockSpec(memory_space=pltpu.VMEM),
        scratch_shapes=[
            pltpu.VMEM((2, rows, width), BF16),
            pltpu.VMEM(slice_gates.shape[1:], BF16),
            pltpu.VMEM(last_gate.shape, BF16),
            pltpu.SMEM(mix_first.shape, F32),
            pltpu.SMEM(mix_second.shape, F32),
            pltpu.SMEM(mix_joint.shape, F32),
            pltpu.VMEM((2, 8 * part, 2 * width), BF16),
            pltpu.VMEM((2, 8 * part, 2 * width), BF16),
            pltpu.VMEM((8, part, 2 * width), BF16),
            pltpu.VMEM((8, part, 2 * width), BF16),
            pltpu.VMEM((na, part, 2 * width), BF16),
            pltpu.VMEM((na, part, 2 * width), BF16),
            pltpu.VMEM((na, nb, part, 2 * width), BF16),
            pltpu.VMEM((na, na - 1, part, 2 * width), BF16),
            dma((8,)), dma((2, 2)), dma((2, 2)), dma((8,)), dma((8,)),
            dma((na,)), dma((na,)), dma((na, na - 1)), dma((na, na - 1)),
        ],
        compiler_params=pltpu.CompilerParams(
            collective_id=0, has_side_effects=True, vmem_limit_bytes=56 * 2**20
        ),
    )(slice_tensors, slice_gates, last_gate, mix_first, mix_second, mix_joint)


def solution(mesh):
    placed = (
        P("cuts", None, "bita", "bitb", None, None),
        P("cuts", None, None, None, None),
        P(),
        P(),
        P(),
        P(),
    )
    pairs = (mesh.shape["cuts"], mesh.shape["bita"], mesh.shape["bitb"]) == (4, 4, 2)
    return jax.shard_map(
        by_kernel if pairs else by_collectives,
        mesh=mesh,
        in_specs=placed,
        out_specs=P(None, "bita", "bitb", None, "cuts", None),
        check_vma=False,
    )
```

```python
import functools

import jax
import jax.numpy as jnp
from jax import lax
from jax.experimental import pallas as pl
from jax.experimental.pallas import tpu as pltpu
from jax.sharding import PartitionSpec as P

MESH = pl.DeviceIdType.MESH
BF16 = jnp.bfloat16
F32 = jnp.float32


def mix_group(values, matrix):
    return jnp.einsum("...csm,cd->...dsm", values, matrix, precision=lax.Precision.HIGHEST)


def contract(tensor, gate_pair, mixing):
    products = jnp.einsum(
        "z...k,wkm->zw...m", tensor, gate_pair, preferred_element_type=jnp.float32
    )
    real_part = products[0, 0] - products[1, 1]
    imag_part = products[0, 1] + products[1, 0]
    out_real = mix_group(real_part, mixing[0]) - mix_group(imag_part, mixing[1])
    out_imag = mix_group(real_part, mixing[1]) + mix_group(imag_part, mixing[0])
    return jnp.stack([out_real, out_imag])


def by_collectives(slice_tensors, slice_gates, last_gate, mix_first, mix_second, mix_joint):
    row_count = slice_tensors.shape[4]
    width_k = slice_tensors.shape[5]
    bita_size = lax.axis_size("bita")
    bitb_size = lax.axis_size("bitb")
    joint_size = bita_size * bitb_size
    own_gates = slice_gates[0]
    tensor = slice_tensors.reshape(2, bita_size, row_count // bita_size, width_k)
    tensor = lax.all_to_all(tensor, "bita", split_axis=1, concat_axis=1, tiled=True)
    tensor = contract(tensor, own_gates[0], mix_first).astype(jnp.bfloat16)
    tensor = tensor.reshape(2, bitb_size, row_count // bitb_size, width_k)
    tensor = lax.all_to_all(tensor, "bitb", split_axis=1, concat_axis=1, tiled=True)
    tensor = contract(tensor, own_gates[1], mix_second).astype(jnp.bfloat16)
    tensor = lax.all_to_all(
        tensor.reshape(2, joint_size, row_count // joint_size, width_k),
        ("bita", "bitb"),
        split_axis=1,
        concat_axis=1,
        tiled=True,
    )
    result = contract(tensor, last_gate, mix_joint)
    amplitudes = lax.psum_scatter(result, "cuts", scatter_dimension=2, tiled=True)
    return amplitudes.reshape(2, 1, 1, joint_size, amplitudes.shape[2], width_k)


def dot(a, b):
    return jnp.dot(a, b, preferred_element_type=F32)


def wide(real, imag):
    return (
        jnp.concatenate([real, imag], axis=1),
        jnp.concatenate([-imag, real], axis=1),
    )


def kernel(
    x_hbm, gates_hbm, last_hbm, m1_hbm, m2_hbm, mj_hbm, out_ref,
    x_ref, gates_ref, last_ref, m1_ref, m2_ref, mj_ref,
    send_a, recv_a, send_b, recv_b, send_c, recv_c, send_d, recv_d,
    load_sem, a_send_sem, a_recv_sem, b_send_sem, b_recv_sem,
    c_send_sem, c_recv_sem, d_send_sem, d_recv_sem,
):
    cut = lax.axis_index("cuts")
    bita = lax.axis_index("bita")
    bitb = lax.axis_index("bitb")
    na, nb = 4, 2
    _, rows, width = x_ref.shape
    fine = out_ref.shape[4]
    y, core = cut // 2, lax.rem(cut, 2)
    at_core = y * 2 + (1 - core)
    at_y = (1 - y) * 2 + core
    to_core = (at_core, bita, bitb)
    to_y = (at_y, bita, bitb)
    to_x = (cut, bita, 1 - bitb)
    at_z = [bita, bita + 1 - 2 * lax.rem(bita, 2), lax.rem(bita + 2, na), na - 1 - bita]
    to_z = [(cut, at, bitb) for at in at_z[1:]]

    def load(src, dst, i):
        copy = pltpu.make_async_copy(src, dst, load_sem.at[i])
        copy.start()
        return copy

    load_gates = [load(gates_hbm.at[0, i], gates_ref.at[i], i) for i in (1, 0)]
    load_x = [load(x_hbm.at[0, z, 0, 0], x_ref.at[z], 2 + z) for z in range(2)]
    load_rest = [
        load(src, dst, 4 + i)
        for i, (src, dst) in enumerate((
            (m1_hbm, m1_ref), (m2_hbm, m2_ref), (mj_hbm, mj_ref), (last_hbm, last_ref)
        ))
    ]

    barrier = pltpu.get_barrier_semaphore()
    for device in [to_core, to_y, to_x] + to_z:
        pl.semaphore_signal(barrier, inc=1, device_id=device, device_id_type=MESH)

    for copy in load_gates:
        copy.wait()
    g1 = wide(gates_ref[1, 0], gates_ref[1, 1])
    both = dot(gates_ref[0, 0], g1[0]) + dot(gates_ref[0, 1], g1[1])
    both = both.astype(BF16)
    gate = wide(both[:, :width], both[:, width:])
    for copy in load_x:
        copy.wait()

    halves = (1 - bitb, bitb)
    part = fine

    def product(target):
        parts = []
        for z in range(2):
            pieces = []
            for half in halves:
                for u in range(na):
                    start = u * (rows // na) + half * (rows // na // nb) + target * fine
                    pieces.append(x_ref[z, pl.ds(pl.multiple_of(start, 16), fine), :])
            parts.append(jnp.concatenate(pieces, axis=0))
        return dot(parts[0], gate[0]) + dot(parts[1], gate[1])

    def remote(src, dst, send_sem, recv_sem, device):
        return pltpu.make_async_remote_copy(
            src_ref=src, dst_ref=dst, send_sem=send_sem, recv_sem=recv_sem,
            device_id=device, device_id_type=MESH,
        )

    a_copies, b_copies, c_copies, d_copies = [], {}, [], {}
    for i, target in enumerate(((1 - y) * 2 + (1 - core), y * 2 + (1 - core))):
        send_a[i] = product(target).astype(BF16)
        if i == 0:
            pl.semaphore_wait(barrier, 6)
        for half in range(2):
            rows_half = pl.ds(half * na * part, na * part)
            copy = remote(
                send_a.at[i, rows_half], recv_a.at[i, rows_half],
                a_send_sem.at[i, half], a_recv_sem.at[i, half], to_core,
            )
            copy.start()
            a_copies.append(copy)

    total = product(at_y)
    a_copies[0].wait_recv()
    order = (0, 1, 2, 3, 4, 5, 6, 7)
    for q in order:
        if q == na:
            a_copies[1].wait_recv()
        rows_q = slice(q * part, (q + 1) * part)
        send_b[q] = (total[rows_q] + recv_a[0, rows_q].astype(F32)).astype(BF16)
        copy = remote(send_b.at[q], recv_b.at[q], b_send_sem.at[q], b_recv_sem.at[q], to_y)
        copy.start()
        b_copies[q] = copy
    total = product(cut)
    a_copies[2].wait_recv()
    a_copies[3].wait_recv()
    total = total + recv_a[1].astype(F32)

    def summed(q):
        b_copies[q].wait_recv()
        return total[q * part:(q + 1) * part] + recv_b[q].astype(F32)

    for h in range(na):
        send_c[h] = summed(h).astype(BF16)
        copy = remote(send_c.at[h], recv_c.at[h], c_send_sem.at[h], c_recv_sem.at[h], to_x)
        copy.start()
        c_copies.append(copy)

    for copy in load_rest:
        copy.wait()
    low = lax.rem(bita, 2)
    lanes = na * na * fine
    by_fine = fine.bit_length() - 1
    w_id = lax.broadcasted_iota(jnp.int32, (na * nb, lanes), 0)
    lane = lax.broadcasted_iota(jnp.int32, (na * nb, lanes), 1)
    u_id = lane >> (by_fine + 2)
    d_id = (lane >> by_fine) & 3
    mixed = [jnp.zeros((na * nb, lanes), F32), jnp.zeros((na * nb, lanes), F32)]
    for b in range(nb):
        first, joint = [], []
        for z in range(2):
            a_part = jnp.zeros((na * nb, lanes), F32)
            for d in range(na):
                a_part = jnp.where(d_id == d, m1_ref[z, at_z[d], b * 2 + low], a_part)
            j_part = jnp.zeros((na * nb, lanes), F32)
            for u in range(na):
                for w in range(na * nb):
                    j_part = jnp.where((u_id == u) & (w_id == w), mj_ref[z, u * nb + b, w], j_part)
            first.append(a_part)
            joint.append(j_part)
        mixed[0] += first[0] * joint[0] - first[1] * joint[1]
        mixed[1] += first[0] * joint[1] + first[1] * joint[0]

    same = (
        lax.broadcasted_iota(jnp.int32, (fine, lanes), 1) & (fine - 1)
    ) == lax.broadcasted_iota(jnp.int32, (fine, lanes), 0)
    spread = jnp.concatenate([
        jnp.where(same, mixed[z][w:w + 1], 0.0) for z in range(2) for w in range(na * nb)
    ], axis=0).astype(BF16)
    last = wide(last_ref[0], last_ref[1])

    def d_start(src, h, slot, d):
        copy = remote(
            src, recv_d.at[h, slot - 1], d_send_sem.at[h, slot - 1],
            d_recv_sem.at[h, slot - 1], to_z[d - 1],
        )
        copy.start()
        d_copies[h, slot] = copy

    for h in range(na):
        own = summed(na + h)
        own_r, own_i = own[:, :width], own[:, width:]
        c_copies[h].wait_recv()
        other = recv_c[h].astype(F32)
        other_r, other_i = other[:, :width], other[:, width:]
        for v in range(nb):
            kr, ki = m2_ref[0, bitb, v], m2_ref[1, bitb, v]
            pr, pi = m2_ref[0, 1 - bitb, v], m2_ref[1, 1 - bitb, v]
            send_d[h, v] = jnp.concatenate([
                own_r * kr - own_i * ki + other_r * pr - other_i * pi,
                own_r * ki + own_i * kr + other_r * pi + other_i * pr,
            ], axis=1).astype(BF16)
        for d in ((2, 1) if h < 2 else (3, 2, 1)):
            d_start(send_d.at[h, at_z[d] // 2], h, d, d)
    for h in range(2):
        d_copies[h, 2].wait_recv()
        d_start(recv_d.at[h, 1], h, 3, 1)

    columns = 2 * na * part
    sums = None
    for g in (1, 0):
        pieces = []
        for h in (2 * g, 2 * g + 1):
            for slot in range(1, na):
                if h >= 2 or slot != 2:
                    d_copies[h, slot].wait_recv()
            pieces += [send_d[h, bita // 2]] + [recv_d[h, s] for s in range(na - 1)]
        value = jnp.concatenate(pieces, axis=0)
        more = dot(spread[:, g * columns:(g + 1) * columns], value)
        sums = more if sums is None else sums + more
    count = na * nb * fine
    real = (sums[:count, :width] - sums[count:, width:]).astype(BF16)
    imag = (sums[:count, width:] + sums[count:, :width]).astype(BF16)
    result = dot(real, last[0]) + dot(imag, last[1])
    for z in range(2):
        out_ref[z, 0, 0] = result[:, z * width:(z + 1) * width].reshape(na * nb, fine, width)
    for copy in a_copies + list(b_copies.values()) + c_copies + list(d_copies.values()):
        copy.wait_send()


def by_kernel(slice_tensors, slice_gates, last_gate, mix_first, mix_second, mix_joint):
    rows, width = slice_tensors.shape[4:]
    na, nb, cuts = lax.axis_size("bita"), lax.axis_size("bitb"), lax.axis_size("cuts")
    fine = rows // (na * nb * cuts)
    part = fine
    hbm = pl.BlockSpec(memory_space=pltpu.MemorySpace.HBM)
    dma = pltpu.SemaphoreType.DMA
    return pl.pallas_call(
        kernel,
        out_shape=pltpu.VMEM((2, 1, 1, na * nb, fine, width), F32),
        in_specs=[hbm] * 6,
        out_specs=pl.BlockSpec(memory_space=pltpu.VMEM),
        scratch_shapes=[
            pltpu.VMEM((2, rows, width), BF16),
            pltpu.VMEM(slice_gates.shape[1:], BF16),
            pltpu.VMEM(last_gate.shape, BF16),
            pltpu.SMEM(mix_first.shape, F32),
            pltpu.SMEM(mix_second.shape, F32),
            pltpu.SMEM(mix_joint.shape, F32),
            pltpu.VMEM((2, 8 * part, 2 * width), BF16),
            pltpu.VMEM((2, 8 * part, 2 * width), BF16),
            pltpu.VMEM((8, part, 2 * width), BF16),
            pltpu.VMEM((8, part, 2 * width), BF16),
            pltpu.VMEM((na, part, 2 * width), BF16),
            pltpu.VMEM((na, part, 2 * width), BF16),
            pltpu.VMEM((na, nb, part, 2 * width), BF16),
            pltpu.VMEM((na, na - 1, part, 2 * width), BF16),
            dma((8,)), dma((2, 2)), dma((2, 2)), dma((8,)), dma((8,)),
            dma((na,)), dma((na,)), dma((na, na - 1)), dma((na, na - 1)),
        ],
        compiler_params=pltpu.CompilerParams(
            collective_id=0, has_side_effects=True, vmem_limit_bytes=56 * 2**20
        ),
    )(slice_tensors, slice_gates, last_gate, mix_first, mix_second, mix_joint)


def solution(mesh):
    placed = (
        P("cuts", None, "bita", "bitb", None, None),
        P("cuts", None, None, None, None),
        P(),
        P(),
        P(),
        P(),
    )
    pairs = (mesh.shape["cuts"], mesh.shape["bita"], mesh.shape["bitb"]) == (4, 4, 2)
    return jax.shard_map(
        by_kernel if pairs else by_collectives,
        mesh=mesh,
        in_specs=placed,
        out_specs=P(None, "bita", "bitb", None, "cuts", None),
        check_vma=False,
    )
```
